512 devices in a mesh: dp: 64 (over y, z), tensor: 8 (over x, core).
Axes of the slice: x: 4, y: 4, z: 16, core: 2. Of those that a mesh axis runs over, the one named last changes fastest.
Arguments:
- hidden: bfloat16 [16384, 8192], P('dp', 'tensor'), may hold values from -8 to 8
- norm_gain: float32 [8192], P('tensor'), may hold values from 0.5 to 1.5
- lm_head: bfloat16 [81920, 8192], P('dp', 'tensor'), may hold values from -8 to 8
- loss_count: int32 [64], P('dp'), may hold values from 0 to 6, as said below
- loss_pos: int32 [64, 6], P('dp'), may hold values from 0 to 255, as said below
- targets: int32 [64, 6], P('dp'), may hold values from 0 to 81919
- dest: int32 [64, 6], P('dp'), may hold values from -1 to 191, as said below
Outputs:
- hidden_grad: bfloat16 [16384, 8192], P('dp', 'tensor')
- row_loss: float32 [192], P('dp')
The draws below stay inside these ranges and needn't reach their ends.
Inputs may be any that keep to these rules, and one draw needn't show every extreme that they name: `loss_count`: the counts sum to 192, and some dp index has 6 loss rows. `loss_pos`: in each row the first loss_count entries are distinct positions; later entries are ignored. `dest`: over all live slots every value from 0 to 191 appears exactly once, so each dp index receives exactly 3 rows (row p belongs to dp index p // 3); empty slots hold -1.
All inputs are finite; a program needn't handle non-finite values.
Results may differ from the reference program's by a relative error of at most 0.009.
Values may be sent and summed in bfloat16 or wider, within the bound.
No kernel may reach another device: no remote copies, remote signals or barrier semaphores. Data moves between devices by JAX's collectives and lax.ppermute only.
A program may use at most 64 MiB of HBM per device.

```python
import math
import jax
import jax.numpy as jnp
import numpy as np
from jax import lax

D = 8192
V_DEV = 1280
TOK_DEV = 256
BAL = 3
CAP = 6
TOKENS = 16384
VOCAB = 81920
N_DP = 64
N_TENSOR = 8


def loss_layout(key):
    own_key = jax.random.fold_in(key, 11)
    pair_key, shift_key, score_key, shuffle_key = jax.random.split(own_key, 4)
    order = jax.random.permutation(pair_key, N_DP)
    shift = jax.random.randint(shift_key, (N_DP // 2,), 0, BAL + 1)
    shift = shift.at[0].set(BAL)
    values = jnp.stack([BAL + shift, BAL - shift], axis=1).reshape(-1).astype(jnp.int32)
    counts = jnp.zeros((N_DP,), jnp.int32).at[order].set(values)
    scores = jax.random.randint(score_key, (N_DP, TOK_DEV), 0, 1 << 20) * TOK_DEV + jnp.arange(TOK_DEV)[None, :]
    scores = scores.at[:, TOK_DEV - 1].set(-1)
    scores = scores.at[:, 0].set(-2)
    chosen = jnp.argsort(scores, axis=1)[:, :CAP]
    positions = jnp.sort(chosen, axis=1).astype(jnp.int32)
    shuffled = jax.random.permutation(shuffle_key, N_DP * BAL).astype(jnp.int32)
    starts = jnp.cumsum(counts) - counts
    slots = jnp.arange(CAP, dtype=jnp.int32)
    index = starts[:, None] + slots[None, :]
    live_slots = slots[None, :] < counts[:, None]
    destination = jnp.where(live_slots, shuffled[jnp.minimum(index, N_DP * BAL - 1)], -1).astype(jnp.int32)
    return (counts, positions, destination)


def draw_loss_count(key, part):
    return loss_layout(key)[0]


def draw_loss_pos(key, part):
    return loss_layout(key)[1]


def draw_dest(key, part):
    return loss_layout(key)[2]


def draw_hidden(key, part):
    own_key = jax.random.fold_in(key, 31)
    row_key, column_key, base_key = jax.random.split(own_key, 3)
    row_scale = jnp.exp(jax.random.uniform(row_key, (TOKENS, 1), jnp.float32, 0.0, math.log(10.0)))
    column_block = (jnp.arange(D) // (D // N_TENSOR)).astype(jnp.float32) / (N_TENSOR - 1)
    spread = jnp.exp(jax.random.uniform(column_key, (D,), jnp.float32, 0.0, math.log(6.0)))
    base_draw = jax.random.normal(base_key, (TOKENS, D), jnp.float32)
    columns = spread * jnp.sqrt(1.0 + 2.0 * column_block)
    values = 0.004 * row_scale * columns[None, :] * base_draw
    return jnp.clip(values, -8.0, 8.0).astype(jnp.bfloat16)


def draw_lm_head(key, part):
    own_key = jax.random.fold_in(key, 41)
    scale_key, base_key, shared_key = jax.random.split(own_key, 3)
    vocab_block = (jnp.arange(VOCAB) // V_DEV).astype(jnp.float32) / (N_DP - 1)
    factor = jnp.exp(jax.random.uniform(scale_key, (VOCAB, 1), jnp.float32, math.log(0.7), math.log(1.4)))
    scale = (2.8 + 0.5 * vocab_block)[:, None] * factor / math.sqrt(D)
    base_draw = jax.random.normal(base_key, (VOCAB, D), jnp.float32)
    shared = jax.random.normal(shared_key, (D,), jnp.float32)
    values = scale * base_draw + 0.077 * shared[None, :]
    return jnp.clip(values, -8.0, 8.0).astype(jnp.bfloat16)


def with_ends(drawn, key, least, largest):
    dims = drawn.shape
    spot = [jax.random.randint(jax.random.fold_in(key, axis), (), 0, dims[axis]) for axis in range(len(dims))]
    drawn = drawn.at[tuple(spot)].set(least)
    longest = dims.index(max(dims))
    spot[longest] = (spot[longest] + 1) % dims[longest]
    return drawn.at[tuple(spot)].set(largest)


def ranked_wide(stream_key, dims, number_of, lean):
    portions = [min(1 << octave, number_of + 1 - (1 << octave)) * (1 << 20) // math.isqrt((1 << octave) ** lean) + 1 for octave in range((number_of + 1).bit_length()) if 1 << octave <= number_of]
    scale = 1 + sum(portions) // (1 << 30)
    grid = np.cumsum(np.array([max(1, weight // scale) for weight in portions]))
    pick = jax.random.randint(jax.random.fold_in(stream_key, 1), dims, 0, int(grid[len(portions) - 1]))
    start = jnp.left_shift(1, jnp.searchsorted(jnp.asarray(grid, jnp.int32), pick, side="right").astype(jnp.int32))
    rank = start - 1 + jax.random.randint(jax.random.fold_in(stream_key, 4), dims, 0, 1 << 30) % jnp.minimum(start, number_of + 1 - start)
    return jax.random.permutation(jax.random.fold_in(stream_key, 2), number_of)[rank].astype(jnp.int32)


def setup_inputs(seed: int = 0) -> dict:
    keys = jax.random.split(jax.random.key(seed), 8)
    return {
        "hidden": draw_hidden(jax.random.fold_in(keys[7], 71), 0),
        "norm_gain": jnp.clip(1.0 + 0.1 * jax.random.normal(keys[1], (D,), jnp.float32), 0.5, 1.5),
        "lm_head": draw_lm_head(jax.random.fold_in(keys[7], 71), 0),
        "loss_count": draw_loss_count(jax.random.fold_in(keys[7], 71), 0),
        "loss_pos": draw_loss_pos(jax.random.fold_in(keys[7], 71), 0),
        "targets": with_ends(ranked_wide(keys[5], (N_DP, CAP), VOCAB, 2), jax.random.fold_in(keys[5], 3), 0, VOCAB - 1).astype(jnp.int32),
        "dest": draw_dest(jax.random.fold_in(keys[7], 71), 0),
    }


def reference(hidden, norm_gain, lm_head, loss_count, loss_pos, targets, dest):
    slot_total = N_DP * BAL
    slots = jnp.arange(CAP, dtype=jnp.int32)
    live_slots = slots[None, :] < loss_count[:, None]
    token_index = (jnp.arange(N_DP, dtype=jnp.int32)[:, None] * TOK_DEV + loss_pos).reshape(-1)
    row_place = jnp.where(live_slots, dest, slot_total).reshape(-1)
    row_token = jnp.zeros((slot_total,), jnp.int32).at[row_place].set(token_index, mode='drop')
    row_target = jnp.zeros((slot_total,), jnp.int32).at[row_place].set(targets.reshape(-1), mode='drop')
    raw_rows = hidden[row_token].astype(jnp.float32)
    inverse = lax.rsqrt(lax.optimization_barrier(jnp.mean(raw_rows * raw_rows, axis=1)) + 1e-06)
    normed = (raw_rows * norm_gain[None, :] * inverse[:, None]).astype(jnp.bfloat16)
    logits = jnp.dot(normed, lm_head.T, preferred_element_type=jnp.float32)
    row_top = lax.optimization_barrier(jnp.max(logits, axis=1))
    row_sum = lax.optimization_barrier(jnp.sum(jnp.exp(logits - row_top[:, None]), axis=1))
    log_total = row_top + jnp.log(row_sum)
    picked = jnp.take_along_axis(logits, row_target[:, None], axis=1)[:, 0]
    row_loss = log_total - picked
    target_hit = (jnp.arange(VOCAB, dtype=jnp.int32)[None, :] == row_target[:, None]).astype(jnp.float32)
    grad_logits = (jnp.exp(logits - log_total[:, None]) - target_hit).astype(jnp.bfloat16)
    grad_normed = jnp.dot(grad_logits, lm_head, preferred_element_type=jnp.float32)
    scaled = grad_normed * norm_gain[None, :]
    inner_sum = lax.optimization_barrier(jnp.sum(scaled * raw_rows, axis=1))
    grad_raw = scaled * inverse[:, None] - raw_rows * (inner_sum * inverse * inverse * inverse / D)[:, None]
    grad_rows = grad_raw.astype(jnp.bfloat16)
    hidden_grad = jnp.zeros((TOKENS, D), jnp.bfloat16).at[row_token].set(grad_rows)
    return (hidden_grad, row_loss)
```

```python
import functools

import jax
import jax.numpy as jnp
from jax import lax
from jax.experimental import pallas as pl
from jax.experimental.pallas import tpu as pltpu
from jax.sharding import Mesh, PartitionSpec as P

D = 8192
BAL = 3
CAP = 6
NY, NZ, NX, NC = 4, 16, 4, 2
N_DP = NY * NZ
N_TENSOR = NX * NC
ROWS = N_DP * BAL
SUB = ROWS // N_TENSOR
SLOT = 8
LANES = 128
STAT_ROW, OWN_ROW = 6, 7
N_STAT = 5
N_PIECE = 3 * N_STAT

VMEM = pl.BlockSpec(memory_space=pltpu.VMEM)
SMEM = pl.BlockSpec(memory_space=pltpu.SMEM)
HBM = pl.BlockSpec(memory_space=pltpu.HBM)
PARAMS = pltpu.CompilerParams(vmem_limit_bytes=24 * 1024 * 1024)
SMALL = pltpu.CompilerParams(vmem_limit_bytes=4 * 1024 * 1024)
f32, bf16, i32 = jnp.float32, jnp.bfloat16, jnp.int32


def dot(a, b, dims):
    return lax.dot_general(a, b, (dims, ((), ())), preferred_element_type=f32)


def pieces(x):
    hi = x.astype(bf16)
    rest = x - hi.astype(f32)
    mid = rest.astype(bf16)
    low = (rest - mid.astype(f32)).astype(bf16)
    return hi.astype(f32), mid.astype(f32), low.astype(f32)


def pick_kernel(hidden, count_in, pos_in, targets_in, dest_in, out, copies_out, count, pos, targets, dest, rows, sems):
    scalars = []
    for k, (src, dst) in enumerate(((pos_in, pos), (count_in, count), (targets_in, targets), (dest_in, dest))):
        scalars.append(pltpu.make_async_copy(src, dst, sems.at[CAP + k]))
        scalars[-1].start()
    scalars[0].wait()
    copies = []
    for s in range(CAP):
        start = pl.multiple_of(jnp.clip(pos[0, s], 0, 255) // 16 * 16, 16)
        copies.append(pltpu.make_async_copy(hidden.at[pl.ds(start, 16), :], rows.at[s], sems.at[s]))
        copies[-1].start()
    for copy in scalars[1:]:
        copy.wait()
    lane = lax.broadcasted_iota(i32, (1, LANES), 1)
    meta = jnp.zeros((1, LANES), f32)
    for s in range(CAP):
        live = s < count[0]
        t = targets[0, s]
        place = jnp.where(live, dest[0, s], -1)
        digits = (t // 65536, t // 256 % 256, t % 256, place)
        for k, digit in enumerate(digits):
            meta = jnp.where(lane == k * SLOT + s, digit.astype(f32), meta)
    sub8 = lax.broadcasted_iota(i32, (SLOT, 1), 0)
    sub16 = lax.broadcasted_iota(i32, (16, 1), 0)
    total = jnp.where(
        sub8 == STAT_ROW,
        jnp.concatenate([meta, jnp.zeros((1, out.shape[1] - LANES), f32)], axis=1),
        0.0,
    )
    for s in range(CAP):
        copies[s].wait()
        one = jnp.where(sub16 == jnp.clip(pos[0, s], 0, 255) % 16, rows[s].astype(f32), 0.0)
        row = jnp.sum(one, axis=0, keepdims=True)
        total = jnp.where(sub8 == s, row, total)
    out[...] = total.astype(bf16)
    copies_out[...] = jnp.concatenate([total] * NZ, axis=0).astype(bf16)


def column(rows8, k):
    lane = lax.broadcasted_iota(i32, (1, SLOT, LANES), 2)
    sub = lax.broadcasted_iota(i32, (1, SLOT, LANES), 1)
    return jnp.sum(jnp.where(lane == k * SLOT + sub, rows8, 0.0), axis=2, keepdims=True)


def logits_kernel(x0, x1, x2, x3, gain, head_in, part, want, spread, head, sem):
    load = pltpu.make_async_copy(head_in, head, sem)
    load.start()
    y = lax.axis_index("y")
    lane = lax.broadcasted_iota(i32, (1, LANES), 1)
    row_lane = lax.broadcasted_iota(i32, (1, ROWS), 1).astype(f32)
    sub = lax.broadcasted_iota(i32, (NZ, SLOT, 1), 1)
    count = NZ * SLOT
    rows = jnp.zeros((ROWS, gain.shape[1]), f32)
    digits = jnp.zeros((ROWS, LANES), f32)
    dests = []
    for x in (x0, x1, x2, x3):
        meta = x[:, :LANES].astype(f32).reshape(NZ, SLOT, LANES)
        meta = jnp.broadcast_to(meta[:, STAT_ROW : STAT_ROW + 1, :], meta.shape)
        dests.append(jnp.where(sub < CAP, column(meta, 3), -1.0).reshape(count, 1))
        hot = (dests[-1] == row_lane).astype(f32).astype(bf16)
        digit = jnp.zeros((count, LANES), f32)
        for k in range(3):
            digit = jnp.where(lane == k, column(meta, k).reshape(count, 1), digit)
        rows = rows + dot(hot, x[...], ((0,), (0,)))
        digits = digits + dot(hot, digit.astype(bf16), ((0,), (0,)))
    target = digits[:, 0:1] * 65536.0 + digits[:, 1:2] * 256.0 + digits[:, 2:3]
    want[...] = jnp.broadcast_to(target, want.shape)
    for other in range(NY):
        dest = dests[0]
        for k in range(1, NY):
            dest = jnp.where((y + k) % NY == other, dests[k], dest)
        spread[other * count : (other + 1) * count, :] = (dest == row_lane).astype(f32).astype(bf16)
    scaled = (rows * gain[...]).astype(bf16)
    vocab = head.shape[0]
    load.wait()
    part[:, :vocab] = dot(scaled, head[...], ((1,), (1,)))
    part[:, vocab:] = jnp.broadcast_to(
        jnp.sum(rows * rows, axis=1, keepdims=True), (ROWS, LANES)
    )


def vocab_ids(vocab):
    start = (lax.axis_index("y") * NZ + lax.axis_index("z")) * vocab
    return (lax.broadcasted_iota(i32, (1, vocab), 1) + start).astype(f32)


def target_kernel(vocab, head, want, spread, out):
    hit = (vocab_ids(vocab) == want[:, 0:1]).astype(f32).astype(bf16)
    hits = dot(hit, head[...], ((1,), (0,))).astype(bf16)
    rows = dot(spread[...], hits, ((1,), (0,))).reshape(NY, NZ, SLOT, head.shape[1])
    for z in range(NZ):
        block = jnp.concatenate([rows[y, z] for y in range(NY)], axis=0)
        out[z * NY * SLOT : (z + 1) * NY * SLOT, :] = block.astype(bf16)


def softmax_kernel(vocab, parts, want, out):
    total = parts[0:SUB, :]
    for t in range(1, N_TENSOR):
        total = total + parts[t * SUB : (t + 1) * SUB, :]
    inverse = lax.rsqrt(total[:, vocab : vocab + 1] / D + 1e-6)
    logits = total[:, :vocab] * inverse
    rank = lax.axis_index("x") * NC + lax.axis_index("core")
    target = want[pl.ds(pl.multiple_of(rank * SUB, SUB), SUB), :][:, 0:1]
    ids = vocab_ids(vocab)
    top = jnp.max(logits, axis=1, keepdims=True)
    down = logits - top
    weight = jnp.exp(down)
    total_w = jnp.sum(weight, axis=1, keepdims=True)
    total_u = jnp.sum(weight * down, axis=1, keepdims=True)
    hit = jnp.sum(jnp.where(ids == target, logits, 0.0), axis=1, keepdims=True)
    lane = lax.broadcasted_iota(i32, (1, LANES), 1)
    stats = jnp.zeros((SUB, LANES), f32)
    for q, value in enumerate((top, total_w, total_u, hit, inverse)):
        for j, piece in enumerate(pieces(value)):
            stats = jnp.where(lane == 3 * q + j, piece, stats)
    out[:, :vocab] = weight.astype(bf16)
    out[:, vocab:] = stats.astype(bf16)


def as_row(columns):
    lane = lax.broadcasted_iota(i32, (1, SLOT, LANES), 2)
    sub = lax.broadcasted_iota(i32, (1, SLOT, LANES), 1)
    total = jnp.zeros(columns.shape, f32)
    for k in range(N_PIECE):
        total = jnp.where(lane == k * SLOT + sub, columns[:, :, k : k + 1], total)
    return jnp.sum(total, axis=1, keepdims=True)


def grad_kernel(vocab, weights, head, spread, out):
    width = head.shape[1]
    grads = dot(weights[:, :vocab], head[...], ((1,), (0,))).astype(bf16)
    stats = weights[:, vocab:]
    hot = spread[...]
    own = lax.broadcasted_iota(i32, (N_DP * SLOT, 1), 0)
    own = jnp.where(own % SLOT < BAL, own // SLOT * BAL + own % SLOT, -1)
    own_hot = (own == lax.broadcasted_iota(i32, (1, ROWS), 1)).astype(f32).astype(bf16)
    slot_stats = dot(hot, stats, ((1,), (0,))).reshape(N_DP, SLOT, LANES)
    own_stats = dot(own_hot, stats, ((1,), (0,))).reshape(N_DP, SLOT, LANES)
    sub = lax.broadcasted_iota(i32, (1, SLOT, 1), 1)
    slot_grads = dot(hot, grads, ((1,), (0,)))
    first = slot_grads[:, :LANES].reshape(N_DP, SLOT, LANES)
    first = jnp.where(sub == STAT_ROW, as_row(slot_stats), first)
    first = jnp.where(sub == OWN_ROW, as_row(own_stats), first)
    out[:, :LANES] = first.reshape(N_DP * SLOT, LANES).astype(bf16)
    out[:, LANES:] = slot_grads[:, LANES:].astype(bf16)


def read_stats(rows, at):
    rows = jnp.broadcast_to(rows[:, at : at + 1, :], rows.shape)
    out = []
    for q in range(N_STAT):
        out.append(column(rows, 3 * q) + column(rows, 3 * q + 1) + column(rows, 3 * q + 2))
    return out


def merge_stats(stats):
    top = functools.reduce(jnp.maximum, [st[0] for st in stats])
    factors = [jnp.exp(st[0] - top) for st in stats]
    total = sum(f * st[1] for f, st in zip(factors, stats))
    total_u = sum(f * (st[2] + st[1] * (st[0] - top)) for f, st in zip(factors, stats))
    hit = sum(st[3] for st in stats)
    return factors, (top, total, total_u, hit, stats[0][4])


def stats_row(stats):
    lane = lax.broadcasted_iota(i32, (1, 1, LANES), 2)
    columns = jnp.zeros(stats[0].shape[:2] + (LANES,), f32)
    for q, value in enumerate(stats):
        for j, piece in enumerate(pieces(value)):
            columns = jnp.where(lane == 3 * q + j, piece, columns)
    return as_row(columns)


def merge_kernel(parts, out):
    width = parts.shape[1]
    size = parts.shape[0] // NY
    blocks = size // SLOT
    slot_stats, own_stats = [], []
    for r in range(NY):
        heads = parts[r * size : (r + 1) * size, :LANES].astype(f32).reshape(blocks, SLOT, LANES)
        slot_stats.append(read_stats(heads, STAT_ROW))
        own_stats.append(read_stats(heads, OWN_ROW))
    factors, merged = merge_stats(slot_stats)
    _, own_merged = merge_stats(own_stats)
    row, own_row = stats_row(merged), stats_row(own_merged)
    sub = lax.broadcasted_iota(i32, (1, SLOT, 1), 1)
    factors = [factor.reshape(size, 1) for factor in factors]
    for c in range(0, width, LANES):
        grads = jnp.zeros((size, LANES), f32)
        for r in range(NY):
            grads = grads + factors[r] * parts[r * size : (r + 1) * size, c : c + LANES].astype(f32)
        if c == 0:
            grads = grads.reshape(blocks, SLOT, LANES)
            grads = jnp.where(sub == STAT_ROW, row, grads)
            grads = jnp.where(sub == OWN_ROW, own_row, grads).reshape(size, LANES)
        out[:, c : c + LANES] = grads.astype(bf16)


def final_kernel(parts, hits, gain, picked, count, pos, out, loss):
    width = parts.shape[1]
    heads = parts[:, :LANES].astype(f32).reshape(NZ, SLOT, LANES)
    slot_all = read_stats(heads, STAT_ROW)
    own_all = read_stats(heads, OWN_ROW)
    factors, (top, total, total_u, hit, inverse) = merge_stats(
        [[value[z : z + 1] for value in slot_all] for z in range(NZ)]
    )
    _, own = merge_stats([[value[z : z + 1] for value in own_all] for z in range(NZ)])
    sub = lax.broadcasted_iota(i32, (SLOT, 1), 0)
    live = sub < count[0]
    safe = jnp.where(live, total[0], 1.0)
    inner = (total_u[0] / safe + top[0] - hit[0]) * inverse[0] * inverse[0] / D
    losses = own[0][0] + jnp.log(jnp.where(sub < BAL, own[1][0], 1.0)) - own[3][0]
    for i in range(BAL):
        loss[i] = jnp.sum(jnp.where(sub == i, losses, 0.0))
    token = lax.broadcasted_iota(i32, (out.shape[0], 1), 0)
    lane = lax.broadcasted_iota(i32, (1, SLOT), 1)
    hot = jnp.zeros((out.shape[0], SLOT), jnp.bool_)
    for s in range(CAP):
        hot = hot | ((lane == s) & (token == pos[0, s]) & (s < count[0]))
    hot = hot.astype(f32).astype(bf16)
    grads = jnp.zeros((SLOT, width), f32)
    pieces_z = parts[...].astype(f32).reshape(NZ, SLOT, width)
    for z in range(NZ):
        grads = grads + factors[z][0] * pieces_z[z]
    hit_rows = jnp.sum(hits[...].astype(f32).reshape(NY, SLOT, width), axis=0)
    grads = (grads / safe - hit_rows) * gain[...]
    rows = grads * inverse[0] - picked[...].astype(f32) * inner
    rows = jnp.where(live, rows, 0.0).astype(bf16)
    out[...] = dot(hot, rows, ((1,), (0,))).astype(bf16)


def per_device(hidden, norm_gain, lm_head, loss_count, loss_pos, targets, dest):
    vocab, width = lm_head.shape
    tokens = hidden.shape[0]
    gain = norm_gain.reshape(1, width)
    shape = jax.ShapeDtypeStruct
    picked, copies = pl.pallas_call(
        pick_kernel,
        out_shape=(shape((SLOT, width), bf16), shape((NZ * SLOT, width), bf16)),
        in_specs=[HBM] * 5,
        out_specs=(VMEM, VMEM),
        scratch_shapes=[
            pltpu.SMEM((1,), i32),
            pltpu.SMEM((1, CAP), i32),
            pltpu.SMEM((1, CAP), i32),
            pltpu.SMEM((1, CAP), i32),
            pltpu.VMEM((CAP, 16, width), bf16),
            pltpu.SemaphoreType.DMA((CAP + 4,)),
        ],
        compiler_params=SMALL,
        name="pick_rows",
    )(hidden, loss_count, loss_pos, targets, dest)
    rows = lax.all_to_all(copies, "z", 0, 0, tiled=True)
    others = [lax.ppermute(rows, "y", [((i + k) % NY, i) for i in range(NY)]) for k in range(1, NY)]
    part, want, spread = pl.pallas_call(
        logits_kernel,
        out_shape=(
            shape((ROWS, vocab + LANES), f32),
            shape((ROWS, LANES), f32),
            shape((N_DP * SLOT, ROWS), bf16),
        ),
        in_specs=[VMEM] * 5 + [HBM],
        out_specs=(VMEM, VMEM, VMEM),
        scratch_shapes=[pltpu.VMEM((vocab, width), bf16), pltpu.SemaphoreType.DMA(())],
        compiler_params=PARAMS,
        name="partial_logits",
    )(rows, *others, gain, lm_head)
    hits = pl.pallas_call(
        functools.partial(target_kernel, vocab),
        out_shape=shape((N_DP * SLOT, width), bf16),
        in_specs=[VMEM] * 3,
        out_specs=VMEM,
        compiler_params=PARAMS,
        name="target_rows",
    )(lm_head, want, spread)
    hits = lax.psum_scatter(hits, "z", scatter_dimension=0, tiled=True)
    hits = lax.all_to_all(hits, "y", 0, 0, tiled=True)
    parts = lax.all_to_all(part, ("x", "core"), 0, 0, tiled=True)
    weights = pl.pallas_call(
        functools.partial(softmax_kernel, vocab),
        out_shape=shape((SUB, vocab + LANES), bf16),
        in_specs=[VMEM] * 2,
        out_specs=VMEM,
        compiler_params=PARAMS,
        name="local_softmax",
    )(parts, want)
    weights = lax.all_gather(weights, ("x", "core"), axis=0, tiled=True)
    blocks = pl.pallas_call(
        functools.partial(grad_kernel, vocab),
        out_shape=shape((N_DP * SLOT, width), bf16),
        in_specs=[VMEM] * 3,
        out_specs=VMEM,
        compiler_params=PARAMS,
        name="partial_grads",
    )(weights, lm_head, spread)
    blocks = lax.all_to_all(blocks, "y", 0, 0, tiled=True)
    blocks = pl.pallas_call(
        merge_kernel,
        out_shape=shape((NZ * SLOT, width), bf16),
        in_specs=[VMEM],
        out_specs=VMEM,
        compiler_params=PARAMS,
        name="merge_y",
    )(blocks)
    blocks = lax.all_to_all(blocks, "z", 0, 0, tiled=True)
    hidden_grad, row_loss = pl.pallas_call(
        final_kernel,
        out_shape=(shape((tokens, width), bf16), shape((BAL,), f32)),
        in_specs=[VMEM, VMEM, VMEM, VMEM, SMEM, SMEM],
        out_specs=(VMEM, SMEM),
        compiler_params=PARAMS,
        name="merge_z",
    )(blocks, hits, gain, picked, loss_count, loss_pos)
    return hidden_grad, row_loss


def solution(mesh):
    wide = Mesh(mesh.devices.reshape(NY, NZ, NX, NC), ("y", "z", "x", "core"))
    dp, tensor = ("y", "z"), ("x", "core")
    return jax.shard_map(
        per_device,
        mesh=wide,
        in_specs=(
            P(dp, tensor),
            P(tensor),
            P(dp, tensor),
            P(dp),
            P(dp, None),
            P(dp, None),
            P(dp, None),
        ),
        out_specs=(P(dp, tensor), P(dp)),
        check_vma=False,
    )
```
